32 devices in a mesh: dp: 8 (over z, core), tensor: 4 (over y, x).
Axes of the slice: x: 2, y: 2, z: 4, core: 2. Of those that a mesh axis runs over, the one named last changes fastest.
Arguments:
- attention: bfloat16 [4096, 4096], P('dp', 'tensor'), may hold values from -6 to 6
- code_blocks: bfloat16 [4096, 4096], P('tensor'), may hold values from -4 to 4
- block_scales: float32 [32, 32], P('tensor'), may hold values from 0.008 to 0.032
- residual: bfloat16 [4096, 4096], P('dp', 'tensor'), may hold values from -6 to 6
- low_feature: bfloat16 [4096, 4096], P('dp', 'tensor'), may hold values from -6 to 6
- mid_feature: bfloat16 [4096, 4096], P('dp', 'tensor'), may hold values from -6 to 6
- join_weight: bfloat16 [4096, 3, 4096], P('dp', None, 'tensor'), may hold values from -0.0546875 to 0.0546875
- draft_gain: float32 [3, 4096], replicated, may hold values from 0.5 to 2
- cotangent: bfloat16 [3, 4096, 4096], P(None, ('dp', 'tensor')), may hold values from -6 to 6
- loss_mask: int32 [4096], P(('dp', 'tensor')), may hold values 0 or 1
Outputs:
- grad_join: float32 [4096, 3, 4096], P('dp', None, 'tensor')
- grad_gain: float32 [3, 4096], replicated
The draws below stay inside these ranges and needn't reach their ends.
All inputs are finite; a program needn't handle non-finite values. No bound on the sum of `loss_mask` on one device may be relied on, other than what follows from the above.
Results may differ from the reference program's by a relative error of at most 0.023.
Values may be sent and summed in bfloat16 or wider, within the bound.
A program may use at most 128 MiB of HBM per device.

```python
import math
import jax
import jax.numpy as jnp
from jax import lax

D = 4096
ATTN_W = 4096
BLOCK = 128
STEPS = 3
TOK_DEV = 512
TOKENS = 4096
N_DP = 8
N_TENSOR = 4


def place_ends(entries, own_key, least, largest):
    index_at = [jax.random.randint(jax.random.fold_in(own_key, axis), (), 0, length) for axis, length in enumerate(entries.shape)]
    widest = entries.shape.index(max(entries.shape))
    neighbour = index_at[:widest] + [(index_at[widest] + 1) % entries.shape[widest]] + index_at[widest + 1:]
    return entries.at[tuple(index_at)].set(least).at[tuple(neighbour)].set(largest)


def spiked(entries, own_key, source, target, blocks, factor):
    def block_of(position):
        return (jnp.arange(entries.shape[position]) // (entries.shape[position] // blocks)).reshape((-1,) + (1,) * (entries.ndim - 1 - position))

    first = jax.random.permutation(own_key, blocks)[block_of(target)]
    other_side = (block_of(target) + blocks // 2) % blocks
    return jnp.where((block_of(source) == first) | (block_of(source) == other_side), factor * entries, entries)


def shard_levels(key, extent, pieces, smallest, largest):
    level, own = 1.0, jax.random.fold_in(key, 6)
    for position, blocks in pieces:
        draws = jnp.exp(jax.random.uniform(jax.random.fold_in(own, position), (blocks,), jnp.float32, smallest / len(pieces), largest / len(pieces)))
        level = level * jnp.repeat(draws, extent[position] // blocks).reshape([-1 if axis == position else 1 for axis in range(len(extent))])
    return level


def noise(rng, shape, scale, limit, cuts=(), dtype=jnp.bfloat16):
    entries = jax.random.normal(rng, shape, jnp.float32) * scale
    if len(cuts) > 0:
        entries = shard_levels(rng, shape, cuts, -0.22, 0.18) * entries
    return jnp.clip(entries, min=-limit, max=limit).astype(dtype)


def heavy_noise(stream_key, extent, scale, limit, cuts, heavy, kind=jnp.bfloat16):
    entries = scale * jax.random.normal(stream_key, extent, jnp.float32)
    if cuts:
        entries = entries * shard_levels(stream_key, extent, cuts, -0.22, 0.18)
    return jnp.clip(spiked(entries, jax.random.fold_in(stream_key, 3), *heavy), -limit, limit).astype(kind)


def setup_inputs(seed: int = 0) -> dict:
    streams_of = jax.random.split(jax.random.key(seed), 11)
    return {
        "attention": noise(streams_of[0], (TOKENS, ATTN_W), 1.0, 6.0, ((0, 8), (1, 4))),
        "code_blocks": noise(streams_of[1], (ATTN_W, D), 1.0, 4.0, ((0, 4),)),
        "block_scales": jnp.clip(jnp.exp(math.log(0.032) - 1.3862944 * jax.random.uniform(streams_of[2], (ATTN_W // BLOCK, D // BLOCK), jnp.float32) ** shard_levels(streams_of[2], (ATTN_W // BLOCK, D // BLOCK), ((0, 4),), -0.2, 0.2)), 0.008, 0.032),
        "residual": noise(streams_of[3], (TOKENS, D), 1.0, 6.0, ((0, 8), (1, 4))),
        "low_feature": noise(streams_of[4], (TOKENS, D), 1.0, 6.0, ((0, 8), (1, 4))),
        "mid_feature": noise(streams_of[5], (TOKENS, D), 1.0, 6.0, ((0, 8), (1, 4))),
        "join_weight": noise(streams_of[6], (D, 3, D), (3 * D) ** -0.5, 0.0546875, ((0, 8), (2, 4))),
        "draft_gain": jnp.clip(jnp.exp(jax.random.uniform(streams_of[7], (STEPS, D), jnp.float32, math.log(0.5), math.log(2.0))), 0.5, 2.0),
        "cotangent": heavy_noise(streams_of[8], (STEPS, TOKENS, D), 1.0, 6.0, ((1, 32),), (1, 2, 32, 2.75)),
        "loss_mask": place_ends((jax.random.randint(streams_of[9], (TOKENS,), 0, 4) < 3).astype(jnp.int32), jax.random.fold_in(streams_of[9], 1), 0, 1),
    }


EPS = 1e-05

def project_heads(attention, code_blocks, block_scales):
    summed = jnp.zeros((attention.shape[0], code_blocks.shape[1]), jnp.float32)
    for block_index in range(attention.shape[1] // BLOCK):
        lower = block_index * BLOCK
        product = jnp.dot(attention[:, lower:lower + BLOCK], code_blocks[lower:lower + BLOCK], preferred_element_type=jnp.float32)
        summed = summed + product * jnp.repeat(block_scales[block_index], BLOCK)[None, :]
    return summed

def draft_loss(joined_sum, gain_table, cotangent, token_mask, loss_scale):
    current = joined_sum
    running = jnp.zeros((), jnp.float32)
    keeper = token_mask.astype(jnp.float32)[:, None]
    for step_index in range(STEPS):
        square_mean = lax.optimization_barrier(jnp.mean(current * current, axis=-1, keepdims=True))
        normed = current * lax.rsqrt(square_mean + EPS) * gain_table[step_index][None, :]
        current = current + jax.nn.silu(normed)
        running = running + jnp.sum(keeper * cotangent[step_index].astype(jnp.float32) * current)
    return running * loss_scale

def rounded(value):
    return lax.optimization_barrier(value.astype(jnp.bfloat16)).astype(jnp.float32)

def reference(attention, code_blocks, block_scales, residual, low_feature, mid_feature, join_weight, draft_gain, cotangent, loss_mask):
    head_rows = ATTN_W // N_TENSOR
    columns = D // N_TENSOR
    projected = jnp.zeros((TOKENS, D), jnp.float32)
    for shard in range(N_TENSOR):
        lower = shard * head_rows
        partial_value = project_heads(attention[:, lower:lower + head_rows], code_blocks[lower:lower + head_rows], block_scales[lower // BLOCK:(lower + head_rows) // BLOCK])
        projected = projected + rounded(partial_value)
    high_feature = (residual.astype(jnp.float32) + projected).astype(jnp.bfloat16)
    joined_sum = jnp.zeros((TOKENS, D), jnp.float32)
    for shard in range(N_TENSOR):
        lower = shard * columns
        features = jnp.concatenate([low_feature[:, lower:lower + columns], mid_feature[:, lower:lower + columns], high_feature[:, lower:lower + columns]], axis=1)
        weights = join_weight[:, :, lower:lower + columns].reshape(D, 3 * columns)
        partial_value = jnp.dot(features, weights.T, preferred_element_type=jnp.float32)
        joined_sum = joined_sum + rounded(partial_value)
    loss_scale = float(TOKENS) ** (-0.5)
    joined_grad, grad_gain = jax.grad(draft_loss, argnums=(0, 1))(joined_sum, draft_gain, cotangent, loss_mask, loss_scale)
    joined_grad = joined_grad.astype(jnp.bfloat16)
    grad_join = jnp.zeros((D, 3, D), jnp.float32)
    for shard in range(N_DP):
        lower = shard * TOK_DEV
        features = jnp.concatenate([low_feature[lower:lower + TOK_DEV], mid_feature[lower:lower + TOK_DEV], high_feature[lower:lower + TOK_DEV]], axis=1)
        grad_block = jnp.dot(joined_grad[lower:lower + TOK_DEV].T, features, preferred_element_type=jnp.float32)
        grad_join = grad_join + rounded(grad_block).reshape(D, 3, D)
    return (grad_join, grad_gain)
```

```python
import jax
import jax.numpy as jnp
from jax import lax
from jax.sharding import PartitionSpec as P

BLOCK = 128
STEPS = 3
PARTS = 2


EPS = 1e-05


def project_heads(attention, code_blocks, block_scales, shares):
    scales = jnp.repeat(jnp.repeat(block_scales, BLOCK, axis=0), BLOCK, axis=1)
    weights = (code_blocks.astype(jnp.float32) * scales).astype(jnp.bfloat16)
    partial_value = jnp.dot(attention, weights, preferred_element_type=jnp.float32)
    partial_value = partial_value.astype(jnp.bfloat16)
    return partial_value.reshape(attention.shape[0], shares, -1).transpose(1, 0, 2)


def draft_loss(joined_sum, gain_table, cotangent, token_mask, loss_scale):
    current = joined_sum
    running = jnp.zeros((), jnp.float32)
    keeper = token_mask.astype(jnp.float32)[:, None]
    for step_index in range(STEPS):
        square_mean = jnp.mean(current * current, axis=-1, keepdims=True)
        normed = current * lax.rsqrt(square_mean + EPS) * gain_table[step_index][None, :]
        current = current + jax.nn.silu(normed)
        running = running + jnp.sum(keeper * cotangent[step_index].astype(jnp.float32) * current)
    return running * loss_scale


def on_device(
    attention,
    code_blocks,
    block_scales,
    residual,
    low_feature,
    mid_feature,
    join_weight,
    draft_gain,
    cotangent,
    loss_mask,
):
    n_dp = lax.axis_size("dp")
    n_tensor = lax.axis_size("tensor")
    tok_dev, width = residual.shape
    own_tokens = loss_mask.shape[0]
    rows = own_tokens // PARTS
    own_out = join_weight.shape[0]
    loss_scale = float(tok_dev * n_dp) ** (-0.5)

    def piece(feature, part):
        grouped = feature.reshape(n_tensor, PARTS, rows, -1)[:, part]
        return grouped.reshape(n_tensor * rows, -1)

    def gathered(own_piece):
        return lax.all_gather(own_piece, "dp", axis=0, tiled=True)

    outer = jnp.concatenate([low_feature, mid_feature], axis=1)
    outer_all = [gathered(piece(outer, part)) for part in range(PARTS)]
    partial_value = project_heads(attention, code_blocks, block_scales, n_tensor)
    own_share = lax.psum_scatter(partial_value, "tensor", scatter_dimension=0, tiled=False)
    high_feature = (residual.astype(jnp.float32) + own_share.astype(jnp.float32)).astype(jnp.bfloat16)
    high_feature, outer_all[0] = lax.optimization_barrier((high_feature, outer_all[0]))
    high_all = [gathered(piece(high_feature, part)) for part in range(PARTS)]

    outer_weight = join_weight[:, :2].reshape(own_out, -1)
    high_weight = join_weight[:, 2]
    gain_grad = jnp.zeros(draft_gain.shape, jnp.float32)
    outer_grad = jnp.zeros((own_out, 2 * width), jnp.float32)
    high_grad = jnp.zeros((own_out, width), jnp.float32)
    joined_own = grad_own = None
    for part in range(PARTS):
        if part > 0:
            high_all[part], joined_own = lax.optimization_barrier((high_all[part], joined_own))
        joined_partial = jnp.dot(
            outer_all[part], outer_weight.T, preferred_element_type=jnp.float32
        ) + jnp.dot(high_all[part], high_weight.T, preferred_element_type=jnp.float32)
        joined_partial = joined_partial.astype(jnp.bfloat16).reshape(n_dp, n_tensor, rows, own_out)
        scattered = lax.psum_scatter(
            joined_partial.transpose(1, 0, 2, 3), "tensor", scatter_dimension=0, tiled=False
        )
        if part > 0:
            scattered, grad_own = lax.optimization_barrier((scattered, grad_own))
        joined_own = lax.all_to_all(scattered, "dp", split_axis=0, concat_axis=0, tiled=True)
        joined_sum = joined_own.transpose(1, 0, 2).reshape(rows, -1).astype(jnp.float32)
        lower = part * rows
        joined_grad, part_gain = jax.grad(draft_loss, argnums=(0, 1))(
            joined_sum,
            draft_gain,
            cotangent[:, lower : lower + rows],
            loss_mask[lower : lower + rows],
            loss_scale,
        )
        gain_grad = gain_grad + part_gain
        grad_own = joined_grad.astype(jnp.bfloat16).reshape(rows, n_dp, own_out).transpose(1, 0, 2)
        grad_own = lax.all_to_all(grad_own, "dp", split_axis=0, concat_axis=0, tiled=True)
        if part == PARTS - 1:
            gain_grad, grad_own = lax.optimization_barrier((gain_grad, grad_own))
        grad_all = lax.all_gather(grad_own, "tensor", axis=0, tiled=False)
        grad_all = grad_all.transpose(1, 0, 2, 3).reshape(-1, own_out)
        contract = (((0,), (0,)), ((), ()))
        outer_grad = outer_grad + lax.dot_general(
            grad_all, outer_all[part], contract, preferred_element_type=jnp.float32
        )
        high_grad = high_grad + lax.dot_general(
            grad_all, high_all[part], contract, preferred_element_type=jnp.float32
        )
    grad_gain = lax.psum(gain_grad, ("dp", "tensor"))
    grad_join = jnp.concatenate(
        [outer_grad.reshape(own_out, 2, width), high_grad[:, None]], axis=1
    )
    return (grad_join, grad_gain)


def solution(mesh):
    return jax.shard_map(
        on_device,
        mesh=mesh,
        in_specs=(
            P("dp", "tensor"),
            P("tensor", None),
            P("tensor", None),
            P("dp", "tensor"),
            P("dp", "tensor"),
            P("dp", "tensor"),
            P("dp", None, "tensor"),
            P(),
            P(None, ("dp", "tensor"), None),
            P(("dp", "tensor")),
        ),
        out_specs=(P("dp", None, "tensor"), P()),
        check_vma=False,
    )
```

```python
import jax
import jax.numpy as jnp
from jax import lax
from jax.sharding import PartitionSpec as P

BLOCK = 128
STEPS = 3
PARTS = 2


EPS = 1e-05


def project_heads(attention, code_blocks, block_scales, shares):
    heads, features = code_blocks.shape
    scales = jnp.repeat(block_scales, BLOCK, axis=1)[:, None, :]
    weights = code_blocks.reshape(-1, BLOCK, features).astype(jnp.float32) * scales
    weights = lax.optimization_barrier(weights.astype(jnp.bfloat16).reshape(heads, features))
    own = features // shares
    return jnp.stack(
        [
            jnp.dot(
                attention,
                weights[:, share * own : (share + 1) * own],
                preferred_element_type=jnp.float32,
            ).astype(jnp.bfloat16)
            for share in range(shares)
        ]
    )


def draft_loss(joined_sum, gain_table, cotangent, token_mask, loss_scale):
    current = joined_sum
    running = jnp.zeros((), jnp.float32)
    keeper = token_mask.astype(jnp.float32)[:, None]
    for step_index in range(STEPS):
        square_mean = jnp.mean(current * current, axis=-1, keepdims=True)
        normed = current * lax.rsqrt(square_mean + EPS) * gain_table[step_index][None, :]
        current = current + jax.nn.silu(normed)
        running = running + jnp.sum(keeper * cotangent[step_index].astype(jnp.float32) * current)
    return running * loss_scale


def on_device(
    attention,
    code_blocks,
    block_scales,
    residual,
    low_feature,
    mid_feature,
    join_weight,
    draft_gain,
    cotangent,
    loss_mask,
):
    n_dp = lax.axis_size("dp")
    n_tensor = lax.axis_size("tensor")
    tok_dev, width = residual.shape
    own_tokens = loss_mask.shape[0]
    rows = own_tokens // PARTS
    own_out = join_weight.shape[0]
    loss_scale = float(tok_dev * n_dp) ** (-0.5)

    def piece(feature, part):
        grouped = feature.reshape(n_tensor, PARTS, rows, -1)[:, part]
        return grouped.reshape(n_tensor * rows, -1)

    def gathered(own_piece):
        return lax.all_gather(own_piece, "dp", axis=0, tiled=True)

    outer = jnp.concatenate([low_feature, mid_feature], axis=1)
    outer_all = [gathered(piece(outer, part)) for part in range(PARTS)]
    partial_value = project_heads(attention, code_blocks, block_scales, n_tensor)
    own_share = lax.psum_scatter(partial_value, "tensor", scatter_dimension=0, tiled=False)
    high_feature = (residual.astype(jnp.float32) + own_share.astype(jnp.float32)).astype(jnp.bfloat16)
    high_feature, outer_all[0] = lax.optimization_barrier((high_feature, outer_all[0]))
    high_all = [gathered(piece(high_feature, part)) for part in range(PARTS)]

    outer_weight = join_weight[:, :2].reshape(own_out, -1)
    high_weight = join_weight[:, 2]
    gain_grad = jnp.zeros(draft_gain.shape, jnp.float32)
    outer_grad = jnp.zeros((own_out, 2 * width), jnp.float32)
    high_grad = jnp.zeros((own_out, width), jnp.float32)
    joined_own = grad_own = None
    high_all[0], *outer_all = lax.optimization_barrier((high_all[0], *outer_all))
    for part in range(PARTS):
        if part > 0:
            high_all[part], joined_own = lax.optimization_barrier((high_all[part], joined_own))
        joined_partial = jnp.dot(
            outer_all[part], outer_weight.T, preferred_element_type=jnp.float32
        ) + jnp.dot(high_all[part], high_weight.T, preferred_element_type=jnp.float32)
        joined_partial = joined_partial.astype(jnp.bfloat16).reshape(n_dp, n_tensor, rows, own_out)
        scattered = lax.psum_scatter(
            joined_partial.transpose(1, 0, 2, 3), "tensor", scatter_dimension=0, tiled=False
        )
        if part > 0:
            scattered, grad_own = lax.optimization_barrier((scattered, grad_own))
        joined_own = lax.all_to_all(scattered, "dp", split_axis=0, concat_axis=0, tiled=True)
        joined_sum = joined_own.transpose(1, 0, 2).reshape(rows, -1).astype(jnp.float32)
        lower = part * rows
        joined_grad, part_gain = jax.grad(draft_loss, argnums=(0, 1))(
            joined_sum,
            draft_gain,
            cotangent[:, lower : lower + rows],
            loss_mask[lower : lower + rows],
            loss_scale,
        )
        gain_grad = gain_grad + part_gain
        grad_own = joined_grad.astype(jnp.bfloat16).reshape(rows, n_dp, own_out).transpose(1, 0, 2)
        grad_own = lax.all_to_all(grad_own, "dp", split_axis=0, concat_axis=0, tiled=True)
        if part == PARTS - 1:
            gain_grad, grad_own = lax.optimization_barrier((gain_grad, grad_own))
        grad_all = lax.all_gather(grad_own, "tensor", axis=0, tiled=False)
        grad_all = grad_all.transpose(1, 0, 2, 3).reshape(-1, own_out)
        contract = (((0,), (0,)), ((), ()))
        outer_grad = outer_grad + lax.dot_general(
            grad_all, outer_all[part], contract, preferred_element_type=jnp.float32
        )
        high_grad = high_grad + lax.dot_general(
            grad_all, high_all[part], contract, preferred_element_type=jnp.float32
        )
    gain_rows = lax.all_gather(gain_grad, "dp", axis=0, tiled=False)
    grad_gain = jnp.sum(lax.all_gather(jnp.sum(gain_rows, axis=0), "tensor", axis=0, tiled=False), axis=0)
    grad_join = jnp.concatenate(
        [outer_grad.reshape(own_out, 2, width), high_grad[:, None]], axis=1
    )
    return (grad_join, grad_gain)


def solution(mesh):
    return jax.shard_map(
        on_device,
        mesh=mesh,
        in_specs=(
            P("dp", "tensor"),
            P("tensor", None),
            P("tensor", None),
            P("dp", "tensor"),
            P("dp", "tensor"),
            P("dp", "tensor"),
            P("dp", None, "tensor"),
            P(),
            P(None, ("dp", "tensor"), None),
            P(("dp", "tensor")),
        ),
        out_specs=(P("dp", None, "tensor"), P()),
        check_vma=False,
    )
```

```python
import jax
import jax.numpy as jnp
from jax import lax
from jax.sharding import PartitionSpec as P

BLOCK = 128
STEPS = 3
PARTS = 2


EPS = 1e-05


def project_heads(attention, code_blocks, block_scales, shares):
    heads, features = code_blocks.shape
    scales = jnp.repeat(block_scales, BLOCK, axis=1)[:, None, :]
    weights = code_blocks.reshape(-1, BLOCK, features).astype(jnp.float32) * scales
    weights = lax.optimization_barrier(weights.astype(jnp.bfloat16).reshape(heads, features))
    own = features // shares
    return jnp.stack(
        [
            jnp.dot(
                attention,
                weights[:, share * own : (share + 1) * own],
                preferred_element_type=jnp.float32,
            ).astype(jnp.bfloat16)
            for share in range(shares)
        ]
    )


def draft_loss(joined_sum, gain_table, cotangent, token_mask, loss_scale):
    current = joined_sum
    running = jnp.zeros((), jnp.float32)
    keeper = token_mask.astype(jnp.float32)[:, None]
    for step_index in range(STEPS):
        square_mean = jnp.mean(current * current, axis=-1, keepdims=True)
        normed = current * lax.rsqrt(square_mean + EPS) * gain_table[step_index][None, :]
        current = current + jax.nn.silu(normed)
        running = running + jnp.sum(keeper * cotangent[step_index].astype(jnp.float32) * current)
    return running * loss_scale


def on_device(
    attention,
    code_blocks,
    block_scales,
    residual,
    low_feature,
    mid_feature,
    join_weight,
    draft_gain,
    cotangent,
    loss_mask,
):
    n_dp = lax.axis_size("dp")
    n_tensor = lax.axis_size("tensor")
    tok_dev, width = residual.shape
    own_tokens = loss_mask.shape[0]
    rows = own_tokens // PARTS
    own_out = join_weight.shape[0]
    loss_scale = float(tok_dev * n_dp) ** (-0.5)

    def piece(feature, part):
        grouped = feature.reshape(n_tensor, PARTS, rows, -1)[:, part]
        return grouped.reshape(n_tensor * rows, -1)

    def gathered(own_piece):
        return lax.all_gather(own_piece, "dp", axis=0, tiled=True)

    low_all = [gathered(piece(low_feature, part)) for part in range(PARTS)]
    mid_all = [gathered(piece(mid_feature, part)) for part in range(PARTS)]
    partial_value = project_heads(attention, code_blocks, block_scales, n_tensor)
    partial_value, low_all[0] = lax.optimization_barrier((partial_value, low_all[0]))
    own_share = lax.psum_scatter(partial_value, "tensor", scatter_dimension=0, tiled=False)
    high_feature = (residual.astype(jnp.float32) + own_share.astype(jnp.float32)).astype(jnp.bfloat16)
    high_all = [gathered(piece(high_feature, part)) for part in range(PARTS)]

    weights = [join_weight[:, kind] for kind in range(3)]
    gain_grad = jnp.zeros(draft_gain.shape, jnp.float32)
    kind_grads = [jnp.zeros((own_out, width), jnp.float32) for _ in weights]
    joined_own = grad_own = grad_all = None
    high_all[0], *low_all = lax.optimization_barrier((high_all[0], *low_all))

    def products(totals, grad_all, part):
        features = (low_all[part], mid_all[part], high_all[part])
        contract = (((0,), (0,)), ((), ()))
        return [
            total
            + lax.dot_general(grad_all, feature, contract, preferred_element_type=jnp.float32)
            for total, feature in zip(totals, features)
        ]

    for part in range(PARTS):
        if part > 0:
            high_all[part], joined_own = lax.optimization_barrier((high_all[part], joined_own))
        features = (low_all[part], mid_all[part], high_all[part])
        joined_partial = sum(
            jnp.dot(feature, weight.T, preferred_element_type=jnp.float32)
            for feature, weight in zip(features, weights)
        )
        joined_partial = joined_partial.astype(jnp.bfloat16).reshape(n_dp, n_tensor, rows, own_out)
        scattered = lax.psum_scatter(
            joined_partial.transpose(1, 0, 2, 3), "tensor", scatter_dimension=0, tiled=False
        )
        if part > 0:
            scattered, grad_own = lax.optimization_barrier((scattered, grad_own))
        joined_own = lax.all_to_all(scattered, "dp", split_axis=0, concat_axis=0, tiled=True)
        joined_sum = joined_own.transpose(1, 0, 2).reshape(rows, -1).astype(jnp.float32)
        lower = part * rows
        joined_grad, part_gain = jax.grad(draft_loss, argnums=(0, 1))(
            joined_sum,
            draft_gain,
            cotangent[:, lower : lower + rows],
            loss_mask[lower : lower + rows],
            loss_scale,
        )
        gain_grad = gain_grad + part_gain
        grad_own = joined_grad.astype(jnp.bfloat16).reshape(rows, n_dp, own_out).transpose(1, 0, 2)
        if part > 0:
            grad_own, grad_all = lax.optimization_barrier((grad_own, grad_all))
            kind_grads = products(kind_grads, grad_all, part - 1)
        grad_own = lax.all_to_all(grad_own, "dp", split_axis=0, concat_axis=0, tiled=True)
        if part == PARTS - 1:
            gain_grad, grad_own = lax.optimization_barrier((gain_grad, grad_own))
        grad_all = lax.all_gather(grad_own, "tensor", axis=0, tiled=False)
        grad_all = grad_all.transpose(1, 0, 2, 3).reshape(-1, own_out)
    kind_grads = products(kind_grads, grad_all, PARTS - 1)
    gain_rows = lax.all_gather(gain_grad, "dp", axis=0, tiled=False)
    grad_gain = jnp.sum(lax.all_gather(jnp.sum(gain_rows, axis=0), "tensor", axis=0, tiled=False), axis=0)
    grad_join = jnp.stack(kind_grads, axis=1)
    return (grad_join, grad_gain)


def solution(mesh):
    return jax.shard_map(
        on_device,
        mesh=mesh,
        in_specs=(
            P("dp", "tensor"),
            P("tensor", None),
            P("tensor", None),
            P("dp", "tensor"),
            P("dp", "tensor"),
            P("dp", "tensor"),
            P("dp", None, "tensor"),
            P(),
            P(None, ("dp", "tensor"), None),
            P(("dp", "tensor")),
        ),
        out_specs=(P("dp", None, "tensor"), P()),
        check_vma=False,
    )
```
